32 devices in a mesh: grp: 2 (over x), obs: 16 (over z, y, core).
Axes of the slice: x: 2, y: 2, z: 4, core: 2. Of those that a mesh axis runs over, the one named last changes fastest.
Arguments:
- anomalies: bfloat16 [512, 16384], P(('grp', 'obs')), parts along dimension 0, may hold values from -6 to 6
- innovations: bfloat16 [512, 16384], P(('grp', 'obs')), parts along dimension 0, may hold values from -6 to 6
- sort_order: int32 [32768], P(('grp', 'obs')), parts along dimension 0, may hold values from 0 to 16383, as said below
- obs_error: float32 [32768], P(('grp', 'obs')), parts along dimension 0, may hold values from 0.2 to 2
Outputs:
- gain_product: float32 [32768, 256], P(('grp', 'obs')), parts along dimension 0
The draws below stay inside these ranges and needn't reach their ends.
There are 2 independent parts, one for each index of `grp`. The reference program is written for one: setup_inputs(seed, part) draws one part's arguments, and reference() takes and returns one part's arrays. A program takes and returns all parts, laid end to end along the dimension named above; each array names one. Nothing has to cross between parts.
Inputs may be any that keep to these rules, and one draw needn't show every extreme that they name: Each acquisition index appears exactly once, and sort_order[p] lies in the same aligned block of 128 positions as p.
All inputs are finite; a program needn't handle non-finite values.
Results may differ from the reference program's by a relative error of at most 0.0025.
Values may be sent and summed in bfloat16 or wider, within the bound.
A program may use at most 64 MiB of HBM per device.

```python
import math
import jax
import jax.numpy as jnp
from jax import lax

M = 256
K = 256
OBS_DEV = 1024
LOC = 512
PERM_BLK = 128
NOBS = 16384


def draw_sort_order(key, part):
    blocks = NOBS // PERM_BLK
    keys = jax.random.split(key, blocks)
    within = jax.vmap(lambda k: jax.random.permutation(k, PERM_BLK))(keys)
    starts = jnp.arange(blocks, dtype=jnp.int32)[:, None] * PERM_BLK
    return (within.astype(jnp.int32) + starts).reshape(NOBS).astype(jnp.int32)


def block_scale(rng, extent, cuts, low, top_value):
    level = 1.0
    for axis_at, blocks in cuts:
        heights = jax.random.uniform(jax.random.fold_in(jax.random.fold_in(rng, 6), axis_at), (blocks,), jnp.float32, low / len(cuts), top_value / len(cuts))
        level = level * jnp.repeat(jnp.exp(heights), extent[axis_at] // blocks).reshape((-1,) + (1,) * (len(extent) - 1 - axis_at))
    return level


def normal_values(rng, dims, spread, bound, cuts=(), held_as=jnp.bfloat16):
    values = spread * jax.random.normal(rng, dims, jnp.float32)
    if cuts:
        values = values * block_scale(rng, dims, cuts, -0.22, 0.18)
    return jnp.clip(values, -bound, bound).astype(held_as)


def setup_inputs(seed: int = 0, part: int = 0) -> dict:
    streams_of = jax.random.split(jax.random.key(seed), 5)
    part_keys = jax.random.split(jax.random.fold_in(streams_of[4], part), 5)
    return {
        "anomalies": normal_values(part_keys[0], (M, NOBS), 1.0, 6.0, ((0, 16),)),
        "innovations": normal_values(part_keys[1], (K, NOBS), 1.0, 6.0, ((0, 16),)),
        "sort_order": draw_sort_order(jax.random.fold_in(jax.random.fold_in(streams_of[4], part), 71), part),
        "obs_error": jnp.clip(jnp.exp(math.log(2.0) - 2.3025851 * jax.random.uniform(part_keys[3], (NOBS,), jnp.float32) ** block_scale(part_keys[3], (NOBS,), ((0, 16),), -0.2, 0.2)), 0.2, 2.0),
    }


def gaspari(z):
    inner = z * z * (z * (z * (-0.25 * z + 0.5) + 0.625) - 5.0 / 3.0) + 1.0
    zs = jnp.maximum(z, 1.0)
    outer = zs * zs * (zs * (zs * (zs / 12.0 - 0.5) + 0.625) + 5.0 / 3.0) - 5.0 * zs + 4.0 - 2.0 / (3.0 * zs)
    return jnp.where(z <= 1.0, inner, jnp.where(z < 2.0, outer, 0.0 * z))


def taper_scale(first_row, rows, cols, offset, half_width, members):
    row_ids = first_row + lax.iota(jnp.int32, rows)
    col_ids = lax.iota(jnp.int32, cols) + offset * cols
    dist = jnp.abs(row_ids[:, None] - col_ids[None, :]).astype(jnp.float32)
    return gaspari(dist / half_width) / (members - 1.0)


def tile_term(y_rows, y_cols, d_cols, offset):
    gram = lax.dot_general(y_rows, y_cols, (((0,), (0,)), ((), ())), preferred_element_type=jnp.float32)
    weights = (gram * taper_scale(0, OBS_DEV, OBS_DEV, offset, LOC * 1.0, M * 1.0)).astype(jnp.bfloat16)
    return lax.dot_general(weights, d_cols, (((1,), (1,)), ((), ())), preferred_element_type=jnp.float32)


def reference(anomalies, innovations, sort_order, obs_error):
    sorted_anom = jnp.take(anomalies, sort_order, axis=1)
    sorted_innov = jnp.take(innovations, sort_order, axis=1)
    tiles = NOBS // OBS_DEV
    y_pan = sorted_anom.reshape(M, tiles, OBS_DEV).transpose(1, 0, 2)
    d_pan = sorted_innov.reshape(K, tiles, OBS_DEV).transpose(1, 0, 2)
    zero_y = jnp.zeros((1, M, OBS_DEV), jnp.bfloat16)
    zero_d = jnp.zeros((1, K, OBS_DEV), jnp.bfloat16)
    y_low = jnp.concatenate([zero_y, y_pan[:-1]], axis=0)
    y_up = jnp.concatenate([y_pan[1:], zero_y], axis=0)
    d_low = jnp.concatenate([zero_d, d_pan[:-1]], axis=0)
    d_up = jnp.concatenate([d_pan[1:], zero_d], axis=0)
    errors = obs_error.reshape(tiles, OBS_DEV)

    def one_tile(pieces):
        y_here, y_below, y_above, d_here, d_below, d_above, err = pieces
        total = tile_term(y_here, y_here, d_here, 0)
        total = total + tile_term(y_here, y_below, d_below, -1)
        total = total + tile_term(y_here, y_above, d_above, 1)
        return total + err[:, None] * d_here.T.astype(jnp.float32)

    result = lax.map(one_tile, (y_pan, y_low, y_up, d_pan, d_low, d_up, errors))
    return result.reshape(NOBS, K)
```

```python
import functools

import jax
import jax.numpy as jnp
from jax import lax
from jax.experimental import pallas as pl
from jax.experimental.pallas import tpu as pltpu
from jax.sharding import PartitionSpec as P


def shifted(shard, axis, by):
    peers = lax.axis_size(axis)
    pairs = [(i, i + by) for i in range(peers) if 0 <= i + by < peers]
    return lax.ppermute(shard, axis, pairs)


def gaspari(z):
    inner = z * z * (z * (z * (-0.25 * z + 0.5) + 0.625) - 5.0 / 3.0) + 1.0
    zs = jnp.maximum(z, 1.0)
    outer = (
        zs * zs * (zs * (zs * (zs / 12.0 - 0.5) + 0.625) + 5.0 / 3.0)
        - 5.0 * zs
        + 4.0
        - 2.0 / (3.0 * zs)
    )
    return jnp.where(z <= 1.0, inner, jnp.where(z < 2.0, outer, 0.0 * z))


def taper_scale(first_row, rows, cols, offset, half_width, members):
    row_ids = first_row + lax.iota(jnp.int32, rows)
    col_ids = lax.iota(jnp.int32, cols) + offset * cols
    dist = jnp.abs(row_ids[:, None] - col_ids[None, :]).astype(jnp.float32)
    return gaspari(dist / half_width) / (members - 1.0)


def permute_blocks(values, selector, width, blocks):
    shaped = values.reshape(values.shape[0], blocks, width)
    moved = jnp.einsum("mbi,bij->mbj", shaped, selector, preferred_element_type=jnp.float32)
    return moved.astype(jnp.bfloat16).reshape(values.shape[0], blocks * width)


def plain_on_device(anomalies, innovations, sort_order, obs_error):
    raw_y, raw_d = (
        lax.all_to_all(anomalies, "obs", split_axis=1, concat_axis=0, tiled=True),
        lax.all_to_all(innovations, "obs", split_axis=1, concat_axis=0, tiled=True),
    )
    members = raw_y.shape[0]
    panel = raw_y.shape[1]
    width = min(128, panel)
    blocks = panel // width
    local_ids = (sort_order % width).reshape(blocks, width)
    selector = (lax.iota(jnp.int32, width)[None, :, None] == local_ids[:, None, :]).astype(
        jnp.bfloat16
    )
    y_here = permute_blocks(raw_y, selector, width, blocks)
    d_here = permute_blocks(raw_d, selector, width, blocks)
    block = min(512, panel)
    half_width = panel // 2 * 1.0

    def tile_rows(first, y_cols, offset):
        row_part = lax.slice_in_dim(y_here, first, first + block, axis=1)
        gram = lax.dot_general(
            row_part, y_cols, (((0,), (0,)), ((), ())), preferred_element_type=jnp.float32
        )
        return (gram * taper_scale(first, block, panel, offset, half_width, members * 1.0)).astype(
            jnp.bfloat16
        )

    def apply_rows(weights, d_cols):
        return lax.dot_general(
            weights, d_cols, (((1,), (1,)), ((), ())), preferred_element_type=jnp.float32
        )

    pieces = []
    low_y, low_d = shifted((y_here, d_here), "obs", 1)
    up_y, up_d = shifted((y_here, d_here), "obs", -1)
    for first in range(0, panel, block):
        acc = apply_rows(tile_rows(first, y_here, 0), d_here)
        acc = acc + apply_rows(tile_rows(first, low_y, -1), low_d)
        acc = acc + apply_rows(tile_rows(first, up_y, 1), up_d)
        pieces.append(acc)
    total = jnp.concatenate(pieces, axis=0)
    return total + obs_error[:, None] * d_here.T.astype(jnp.float32)


TILE = 256
SORT = 128
MESH = pl.DeviceIdType.MESH
NT = (((1,), (1,)), ((), ()))
NN = (((1,), (0,)), ((), ()))


def mm(a, b, dims=NN):
    return lax.dot_general(a, b, dims, preferred_element_type=jnp.float32)


def target_order(n):
    half = n // 2
    order = [half]
    for step in range(1, half):
        order += [half + step, half - step]
    return order


def kernel(
    n, parts,
    y_any, d_any, order_ref, err_ref, out_ref,
    raw, y_ext, d_ext, y_t, weights, table, sel, sel_t, err_col,
    send_sem, recv_sem, own_sem, hsend_sem, hrecv_sem,
):
    me = lax.axis_index("obs")
    rows = y_any.shape[0]
    panel = y_any.shape[1] // n
    members = rows * n
    tiles = panel // TILE
    width = panel // parts
    has_low, has_up = me > 0, me < n - 1
    chunks = [(a, c) for a in range(2) for c in range(parts)]

    barrier = pltpu.get_barrier_semaphore()
    for k in range(1, n):
        pl.semaphore_signal(
            barrier, inc=1, device_id={"obs": lax.rem(me + k, n)}, device_id_type=MESH
        )
    pl.semaphore_wait(barrier, n - 1)

    def member_copy(i, k, owner, source):
        a, c = chunks[i]
        start = pl.multiple_of(owner * panel + c * width, SORT)
        return pltpu.make_async_remote_copy(
            src_ref=(y_any, d_any)[a].at[:, pl.ds(start, width)],
            dst_ref=raw.at[a, source, :, pl.ds(c * width, width)],
            send_sem=send_sem.at[i, k],
            recv_sem=recv_sem.at[i, k],
            device_id={"obs": owner},
            device_id_type=MESH,
        )

    def own_copy(a):
        start = pl.multiple_of(me * panel, SORT)
        return pltpu.make_async_copy(
            (y_any, d_any)[a].at[:, pl.ds(start, panel)], raw.at[a, me], own_sem.at[a]
        )

    def panel_copy(i, up):
        a, c = chunks[i]
        ext = (y_ext, d_ext)[a]
        here = pl.ds(panel + c * width, width)
        there = pl.ds((0 if up else 2 * panel) + c * width, width)
        src, dst = (ext.at[:, here], ext.at[:, there]) if a == 0 else (ext.at[here], ext.at[there])
        return pltpu.make_async_remote_copy(
            src_ref=src,
            dst_ref=dst,
            send_sem=hsend_sem.at[i, up],
            recv_sem=hrecv_sem.at[i, up],
            device_id={"obs": lax.rem(me + (1 if up else n - 1), n)},
            device_id_type=MESH,
        )

    for i in range(len(chunks)):
        for k in target_order(n):
            member_copy(i, k, lax.rem(me + k, n), me).start()
    for a in range(2):
        own_copy(a).start()

    row_id = lax.broadcasted_iota(jnp.int32, (SORT, SORT), 0)
    col_id = lax.broadcasted_iota(jnp.int32, (SORT, SORT), 1)
    for b in range(panel // SORT):
        ids = jnp.broadcast_to(order_ref[b : b + 1, :] & (SORT - 1), (SORT, SORT))
        pick = (row_id == ids).astype(jnp.float32)
        sel[b] = pick.astype(jnp.bfloat16)
        sel_t[b] = pick.T.astype(jnp.bfloat16)
        err = jnp.broadcast_to(err_ref[b : b + 1, :], (SORT, SORT))
        column = jnp.sum(jnp.where(row_id == col_id, err, 0.0), axis=1, keepdims=True)
        err_col[b * SORT : (b + 1) * SORT, :] = jnp.broadcast_to(column, (SORT, SORT))
    r = lax.broadcasted_iota(jnp.int32, (TILE, TILE), 0)
    s = lax.broadcasted_iota(jnp.int32, (TILE, TILE), 1)
    for j in range(2 * tiles + 1):
        dist = jnp.abs(s - r + (j - tiles) * TILE).astype(jnp.float32)
        table[:, j * TILE : (j + 1) * TILE] = gaspari(dist / (panel // 2 * 1.0)) / (
            members - 1.0
        )

    def make_weights(j):
        for t in range(tiles):
            at = j - t
            if 0 <= at <= 2 * tiles:
                cols = slice(at * TILE, (at + 1) * TILE)
                gram = mm(y_t[t * TILE : (t + 1) * TILE, :], y_ext[:, j * TILE : (j + 1) * TILE])
                weights[t, :, cols] = (gram * table[:, cols]).astype(jnp.bfloat16)

    def apply_weights(first, last):
        for t in range(tiles):
            lo, hi = max(first, t), min(last, t + 2 * tiles + 1)
            if lo < hi:
                term = mm(
                    weights[t, :, (lo - t) * TILE : (hi - t) * TILE],
                    d_ext[lo * TILE : hi * TILE, :],
                )
                here = slice(t * TILE, (t + 1) * TILE)
                out_ref[here, :] = out_ref[here, :] + term

    def sort_chunk(i):
        a, c = chunks[i]
        for k in target_order(n):
            member_copy(i, k, me, lax.rem(me + n - k, n)).wait_recv()
        for b in range(c * width // SORT, (c + 1) * width // SORT):
            cols = slice(b * SORT, (b + 1) * SORT)
            ext_at = slice(panel + b * SORT, panel + (b + 1) * SORT)
            block = raw[a, :, :, cols].reshape(members, SORT)
            turned = mm(sel_t[b], block, NT)
            if a == 0:
                y_ext[:, ext_at] = mm(block, sel[b]).astype(jnp.bfloat16)
                y_t[cols, :] = turned.astype(jnp.bfloat16)
            else:
                d_ext[ext_at, :] = turned.astype(jnp.bfloat16)
                out_ref[cols, :] = err_col[cols, 0:1] * turned

    def send_panels(i):
        @pl.when(has_up)
        def _():
            panel_copy(i, 1).start()

        @pl.when(has_low)
        def _():
            panel_copy(i, 0).start()

    for a in range(2):
        own_copy(a).wait()
    for i in range(parts):
        sort_chunk(i)
        send_panels(i)
    for j in range(tiles, 2 * tiles):
        make_weights(j)
    for i in range(parts):
        @pl.when(has_low)
        def _():
            panel_copy(i, 1).wait_recv()

        @pl.when(has_up)
        def _():
            panel_copy(i, 0).wait_recv()

    @pl.when(has_low)
    def _():
        for j in range(tiles):
            make_weights(j)

    @pl.when(has_up)
    def _():
        for j in range(2 * tiles, 3 * tiles):
            make_weights(j)

    for i in range(parts, 2 * parts):
        sort_chunk(i)
        send_panels(i)
    apply_weights(tiles, 2 * tiles)

    @pl.when(has_low)
    def _():
        for i in range(parts, 2 * parts):
            panel_copy(i, 1).wait_recv()
        apply_weights(0, tiles)

    @pl.when(has_up)
    def _():
        for i in range(parts, 2 * parts):
            panel_copy(i, 0).wait_recv()
        apply_weights(2 * tiles, 3 * tiles)

    for i in range(len(chunks)):
        for k in target_order(n):
            member_copy(i, k, lax.rem(me + k, n), me).wait_send()

        @pl.when(has_up)
        def _():
            panel_copy(i, 1).wait_send()

        @pl.when(has_low)
        def _():
            panel_copy(i, 0).wait_send()


def fused_on_device(n, anomalies, innovations, sort_order, obs_error):
    rows, total = anomalies.shape
    panel = total // n
    members = rows * n
    parts = 2
    tiles = panel // TILE
    bf16, f32 = jnp.bfloat16, jnp.float32
    vmem = pl.BlockSpec(memory_space=pltpu.VMEM)
    hbm = pl.BlockSpec(memory_space=pl.ANY)
    return pl.pallas_call(
        functools.partial(kernel, n, parts),
        out_shape=jax.ShapeDtypeStruct((panel, members), f32),
        in_specs=[hbm, hbm, vmem, vmem],
        out_specs=vmem,
        scratch_shapes=[
            pltpu.VMEM((2, n, rows, panel), bf16),
            pltpu.VMEM((members, 3 * panel), bf16),
            pltpu.VMEM((3 * panel, members), bf16),
            pltpu.VMEM((panel, members), bf16),
            pltpu.VMEM((tiles, TILE, (2 * tiles + 1) * TILE), bf16),
            pltpu.VMEM((TILE, (2 * tiles + 1) * TILE), f32),
            pltpu.VMEM((panel // SORT, SORT, SORT), bf16),
            pltpu.VMEM((panel // SORT, SORT, SORT), bf16),
            pltpu.VMEM((panel, SORT), f32),
            pltpu.SemaphoreType.DMA((2 * parts, n)),
            pltpu.SemaphoreType.DMA((2 * parts, n)),
            pltpu.SemaphoreType.DMA((2,)),
            pltpu.SemaphoreType.DMA((2 * parts, 2)),
            pltpu.SemaphoreType.DMA((2 * parts, 2)),
        ],
        compiler_params=pltpu.CompilerParams(
            collective_id=0, has_side_effects=True, vmem_limit_bytes=48 * 1024 * 1024
        ),
    )(
        anomalies,
        innovations,
        sort_order.reshape(panel // SORT, SORT),
        obs_error.reshape(panel // SORT, SORT),
    )


def on_device(n, anomalies, innovations, sort_order, obs_error):
    rows, total = anomalies.shape
    if rows % 16 or (total // n) % (2 * TILE) or (rows * n) % TILE:
        return plain_on_device(anomalies, innovations, sort_order, obs_error)
    return fused_on_device(n, anomalies, innovations, sort_order, obs_error)


def solution(mesh):
    return jax.shard_map(
        functools.partial(on_device, mesh.shape["obs"]),
        mesh=mesh,
        in_specs=(
            P(("grp", "obs"), None),
            P(("grp", "obs"), None),
            P(("grp", "obs")),
            P(("grp", "obs")),
        ),
        out_specs=P(("grp", "obs"), None),
        check_vma=False,
    )
```

```python
import functools

import jax
import jax.numpy as jnp
from jax import lax
from jax.experimental import pallas as pl
from jax.experimental.pallas import tpu as pltpu
from jax.sharding import PartitionSpec as P


def shifted(shard, axis, by):
    peers = lax.axis_size(axis)
    pairs = [(i, i + by) for i in range(peers) if 0 <= i + by < peers]
    return lax.ppermute(shard, axis, pairs)


def gaspari(z):
    inner = z * z * (z * (z * (-0.25 * z + 0.5) + 0.625) - 5.0 / 3.0) + 1.0
    zs = jnp.maximum(z, 1.0)
    outer = (
        zs * zs * (zs * (zs * (zs / 12.0 - 0.5) + 0.625) + 5.0 / 3.0)
        - 5.0 * zs
        + 4.0
        - 2.0 / (3.0 * zs)
    )
    return jnp.where(z <= 1.0, inner, jnp.where(z < 2.0, outer, 0.0 * z))


def taper_scale(first_row, rows, cols, offset, half_width, members):
    row_ids = first_row + lax.iota(jnp.int32, rows)
    col_ids = lax.iota(jnp.int32, cols) + offset * cols
    dist = jnp.abs(row_ids[:, None] - col_ids[None, :]).astype(jnp.float32)
    return gaspari(dist / half_width) / (members - 1.0)


def permute_blocks(values, selector, width, blocks):
    shaped = values.reshape(values.shape[0], blocks, width)
    moved = jnp.einsum("mbi,bij->mbj", shaped, selector, preferred_element_type=jnp.float32)
    return moved.astype(jnp.bfloat16).reshape(values.shape[0], blocks * width)


def plain_on_device(anomalies, innovations, sort_order, obs_error):
    raw_y, raw_d = (
        lax.all_to_all(anomalies, "obs", split_axis=1, concat_axis=0, tiled=True),
        lax.all_to_all(innovations, "obs", split_axis=1, concat_axis=0, tiled=True),
    )
    members = raw_y.shape[0]
    panel = raw_y.shape[1]
    width = min(128, panel)
    blocks = panel // width
    local_ids = (sort_order % width).reshape(blocks, width)
    selector = (lax.iota(jnp.int32, width)[None, :, None] == local_ids[:, None, :]).astype(
        jnp.bfloat16
    )
    y_here = permute_blocks(raw_y, selector, width, blocks)
    d_here = permute_blocks(raw_d, selector, width, blocks)
    block = min(512, panel)
    half_width = panel // 2 * 1.0

    def tile_rows(first, y_cols, offset):
        row_part = lax.slice_in_dim(y_here, first, first + block, axis=1)
        gram = lax.dot_general(
            row_part, y_cols, (((0,), (0,)), ((), ())), preferred_element_type=jnp.float32
        )
        return (gram * taper_scale(first, block, panel, offset, half_width, members * 1.0)).astype(
            jnp.bfloat16
        )

    def apply_rows(weights, d_cols):
        return lax.dot_general(
            weights, d_cols, (((1,), (1,)), ((), ())), preferred_element_type=jnp.float32
        )

    pieces = []
    low_y, low_d = shifted((y_here, d_here), "obs", 1)
    up_y, up_d = shifted((y_here, d_here), "obs", -1)
    for first in range(0, panel, block):
        acc = apply_rows(tile_rows(first, y_here, 0), d_here)
        acc = acc + apply_rows(tile_rows(first, low_y, -1), low_d)
        acc = acc + apply_rows(tile_rows(first, up_y, 1), up_d)
        pieces.append(acc)
    total = jnp.concatenate(pieces, axis=0)
    return total + obs_error[:, None] * d_here.T.astype(jnp.float32)


TILE = 256
SORT = 128
MESH = pl.DeviceIdType.MESH
NT = (((1,), (1,)), ((), ()))
NN = (((1,), (0,)), ((), ()))


def mm(a, b, dims=NN):
    return lax.dot_general(a, b, dims, preferred_element_type=jnp.float32)


def kernel(
    n,
    y_hbm, d_hbm, order_hbm, err_hbm, out_ref,
    raw, y_ext, d_ext, y_t, weights, table, orders, errs, sel, sel_t, err_col,
    send_sem, recv_sem, own_sem, far_send, far_recv, swap_send, swap_recv,
    mate_send, mate_recv, order_sem, small_sem,
):
    me = lax.axis_index("obs")
    rows = y_hbm.shape[0]
    panel = y_hbm.shape[1] // n
    members = rows * n
    tiles = panel // TILE
    half = n // 2
    odd, side = me % 2, (me // 2) % 2
    mine = (me // 4) * 2 + odd
    own_slot = 1 - odd
    partner = me + 2 * odd - 1
    mate = me + 1 - 2 * odd
    has_low, has_up = me > 0, me < n - 1
    has_partner = (me > 0) & (me < n - 1)
    no_partner = (me == 0) | (me == n - 1)
    chunks = [(0, 0), (0, 1), (1, 0), (1, 1)]

    def here(slot):
        return has_low if slot == 0 else has_up

    def device_at(which, j):
        return (j // 2) * 4 + which * 2 + j % 2

    barrier = pltpu.get_barrier_semaphore()
    for k in range(1, n):
        pl.semaphore_signal(
            barrier, inc=1, device_id={"obs": lax.rem(me + k, n)}, device_id_type=MESH
        )
    pl.semaphore_wait(barrier, n - 1)

    def pair_panel(owner, slot):
        return owner - 1 + owner % 2 + slot

    def columns(at):
        return pl.ds(pl.multiple_of(at * panel, TILE), panel)

    def landing(a, slot, source):
        return raw.at[a, source // 4, (source // 2) % 2, source % 2, :, columns(slot)]

    def side_copy(i, k, owner, source):
        a, slot = chunks[i]
        return pltpu.make_async_remote_copy(
            src_ref=(y_hbm, d_hbm)[a].at[:, columns(pair_panel(owner, slot))],
            dst_ref=landing(a, slot, source),
            send_sem=send_sem.at[i, k],
            recv_sem=recv_sem.at[i, k],
            device_id={"obs": owner},
            device_id_type=MESH,
        )

    def own_copy(i):
        a, slot = chunks[i]
        return pltpu.make_async_copy(
            (y_hbm, d_hbm)[a].at[:, columns(pair_panel(me, slot))],
            landing(a, slot, me),
            own_sem.at[i],
        )

    def far_copy(a, owner, source, j):
        return pltpu.make_async_remote_copy(
            src_ref=(y_hbm, d_hbm)[a].at[:, columns(owner)],
            dst_ref=landing(a, 1 - owner % 2, source),
            send_sem=far_send.at[a],
            recv_sem=far_recv.at[a, j],
            device_id={"obs": owner},
            device_id_type=MESH,
        )

    def swap_copy(i, which):
        a, slot = chunks[i]
        part = raw.at[a, :, which, :, :, columns(slot)]
        return pltpu.make_async_remote_copy(
            src_ref=part,
            dst_ref=part,
            send_sem=swap_send.at[i],
            recv_sem=swap_recv.at[i],
            device_id={"obs": partner},
            device_id_type=MESH,
        )

    def mate_copy(a, parity):
        ext = (y_ext, d_ext)[a]
        there = columns(2 * parity)
        if a == 0:
            src, dst = ext.at[:, pl.ds(panel, panel)], ext.at[:, there]
        else:
            src, dst = ext.at[pl.ds(panel, panel)], ext.at[there]
        return pltpu.make_async_remote_copy(
            src_ref=src,
            dst_ref=dst,
            send_sem=mate_send.at[a],
            recv_sem=mate_recv.at[a],
            device_id={"obs": mate},
            device_id_type=MESH,
        )

    def order_copy(slot):
        return pltpu.make_async_remote_copy(
            src_ref=order_hbm,
            dst_ref=orders.at[slot],
            send_sem=order_sem.at[0],
            recv_sem=order_sem.at[1],
            device_id={"obs": partner},
            device_id_type=MESH,
        )

    far_owner = (1 - side) * (n - 1)
    steps = [half // 2]
    for step in range(1, half // 2):
        steps += [half // 2 + step, half // 2 - step]

    order_here = pltpu.make_async_copy(order_hbm, orders.at[own_slot], small_sem.at[0])
    err_here = pltpu.make_async_copy(err_hbm, errs, small_sem.at[1])
    order_here.start()
    err_here.start()

    @pl.when(has_partner)
    def _():
        order_copy(own_slot).start()

    def for_targets(i, act):
        for k in steps:
            owner = device_at(side, lax.rem(mine + k, half))
            if chunks[i][1] == 0:
                @pl.when(owner > 0)
                def _():
                    act(side_copy(i, k, owner, me))
            else:
                @pl.when(owner < n - 1)
                def _():
                    act(side_copy(i, k, owner, me))

    for i, (a, slot) in enumerate(chunks):
        for_targets(i, lambda copy: copy.start())

        @pl.when(here(slot))
        def _():
            own_copy(i).start()

        if slot == 1:
            far_copy(a, far_owner, me, mine).start()

    row_id = lax.broadcasted_iota(jnp.int32, (SORT, SORT), 0)
    col_id = lax.broadcasted_iota(jnp.int32, (SORT, SORT), 1)
    err_here.wait()
    for b in range(panel // SORT):
        err = jnp.broadcast_to(errs[b : b + 1, :], (SORT, SORT))
        column = jnp.sum(jnp.where(row_id == col_id, err, 0.0), axis=1, keepdims=True)
        err_col[b * SORT : (b + 1) * SORT, :] = jnp.broadcast_to(column, (SORT, SORT))
    r = lax.broadcasted_iota(jnp.int32, (TILE, TILE), 0)
    s = lax.broadcasted_iota(jnp.int32, (TILE, TILE), 1)
    for j in range(2 * tiles + 1):
        dist = jnp.abs(s - r + (j - tiles) * TILE).astype(jnp.float32)
        table[:, j * TILE : (j + 1) * TILE] = gaspari(dist / (panel // 2 * 1.0)) / (
            members - 1.0
        )
    order_here.wait()

    @pl.when(has_partner)
    def _():
        order_copy(1 - own_slot).wait_recv()

    for slot in range(2):
        @pl.when(here(slot))
        def _():
            for b in range(panel // SORT):
                ids = jnp.broadcast_to(orders[slot, b : b + 1, :] & (SORT - 1), (SORT, SORT))
                pick = (row_id == ids).astype(jnp.float32)
                sel[slot, b] = pick.astype(jnp.bfloat16)
                sel_t[slot, b] = pick.T.astype(jnp.bfloat16)

    def make_weights(j):
        for t in range(tiles):
            at = j - t
            if 0 <= at <= 2 * tiles:
                cols = slice(at * TILE, (at + 1) * TILE)
                gram = mm(y_t[t * TILE : (t + 1) * TILE, :], y_ext[:, j * TILE : (j + 1) * TILE])
                weights[t, :, cols] = (gram * table[:, cols]).astype(jnp.bfloat16)

    def weights_of(first, last):
        for j in range(first, last):
            make_weights(j)

    def apply_weights(first, last):
        for t in range(tiles):
            lo, hi = max(first, t), min(last, t + 2 * tiles + 1)
            if lo < hi:
                term = mm(
                    weights[t, :, (lo - t) * TILE : (hi - t) * TILE],
                    d_ext[lo * TILE : hi * TILE, :],
                )
                rows_here = slice(t * TILE, (t + 1) * TILE)
                out_ref[rows_here, :] = out_ref[rows_here, :] + term

    def of_partner(act):
        @pl.when((odd == 1) & has_up)
        def _():
            act(2 * tiles, 3 * tiles)

        @pl.when((odd == 0) & has_low)
        def _():
            act(0, tiles)

    def of_mate(act):
        @pl.when(odd == 1)
        def _():
            act(0, tiles)

        @pl.when(odd == 0)
        def _():
            act(2 * tiles, 3 * tiles)

    def gather(i):
        a, slot = chunks[i]

        @pl.when(here(slot))
        def _():
            own_copy(i).wait()
            for k in steps:
                source = device_at(side, lax.rem(mine + half - k, half))
                side_copy(i, k, me, source).wait_recv()

        @pl.when(has_partner)
        def _():
            swap_copy(i, side).start()

    def sort_chunk(i):
        a, slot = chunks[i]

        @pl.when(has_partner)
        def _():
            swap_copy(i, 1 - side).wait_recv()

        @pl.when(no_partner & (own_slot == slot))
        def _():
            for j in range(half):
                far_copy(a, me, device_at(1 - side, j), j).wait_recv()

        @pl.when(here(slot))
        def _():
            for b in range(panel // SORT):
                at = slice(slot * panel + b * SORT, slot * panel + (b + 1) * SORT)
                block = raw[a, :, :, :, :, at].reshape(members, SORT)
                start = pl.multiple_of((odd + slot) * panel + b * SORT, SORT)
                if a == 0:
                    y_ext[:, pl.ds(start, SORT)] = mm(block, sel[slot, b]).astype(jnp.bfloat16)
                else:
                    d_ext[pl.ds(start, SORT), :] = mm(sel_t[slot, b], block, NT).astype(
                        jnp.bfloat16
                    )

        @pl.when(own_slot == slot)
        def _():
            mate_copy(a, odd).start()
            for b in range(panel // SORT):
                cols = slice(b * SORT, (b + 1) * SORT)
                if a == 0:
                    at = slice(slot * panel + b * SORT, slot * panel + (b + 1) * SORT)
                    block = raw[a, :, :, :, :, at].reshape(members, SORT)
                    y_t[cols, :] = mm(sel_t[slot, b], block, NT).astype(jnp.bfloat16)
                else:
                    own = d_ext[panel + b * SORT : panel + (b + 1) * SORT, :]
                    out_ref[cols, :] = err_col[cols, 0:1] * own.astype(jnp.float32)

    gather(0)
    gather(1)
    sort_chunk(0)
    gather(2)
    sort_chunk(1)
    weights_of(tiles, 2 * tiles)
    of_partner(weights_of)
    gather(3)
    mate_copy(0, 1 - odd).wait_recv()
    of_mate(weights_of)
    sort_chunk(2)
    sort_chunk(3)
    apply_weights(tiles, 2 * tiles)
    of_partner(apply_weights)
    mate_copy(1, 1 - odd).wait_recv()
    of_mate(apply_weights)

    for i, (a, slot) in enumerate(chunks):
        for_targets(i, lambda copy: copy.wait_send())
        if slot == 1:
            far_copy(a, far_owner, me, mine).wait_send()
            mate_copy(a, odd).wait_send()

        @pl.when(has_partner)
        def _():
            swap_copy(i, side).wait_send()

    @pl.when(has_partner)
    def _():
        order_copy(own_slot).wait_send()


def fused_on_device(n, anomalies, innovations, sort_order, obs_error):
    rows, total = anomalies.shape
    panel = total // n
    members = rows * n
    tiles = panel // TILE
    blocks = panel // SORT
    half = n // 2
    bf16, f32 = jnp.bfloat16, jnp.float32
    hbm = pl.BlockSpec(memory_space=pltpu.HBM)
    dma = pltpu.SemaphoreType.DMA
    return pl.pallas_call(
        functools.partial(kernel, n),
        out_shape=jax.ShapeDtypeStruct((panel, members), f32),
        in_specs=[hbm] * 4,
        out_specs=pl.BlockSpec(memory_space=pltpu.VMEM),
        scratch_shapes=[
            pltpu.VMEM((2, n // 4, 2, 2, rows, 2 * panel), bf16),
            pltpu.VMEM((members, 3 * panel), bf16),
            pltpu.VMEM((3 * panel, members), bf16),
            pltpu.VMEM((panel, members), bf16),
            pltpu.VMEM((tiles, TILE, (2 * tiles + 1) * TILE), bf16),
            pltpu.VMEM((TILE, (2 * tiles + 1) * TILE), f32),
            pltpu.VMEM((2, blocks, SORT), jnp.int32),
            pltpu.VMEM((blocks, SORT), f32),
            pltpu.VMEM((2, blocks, SORT, SORT), bf16),
            pltpu.VMEM((2, blocks, SORT, SORT), bf16),
            pltpu.VMEM((panel, SORT), f32),
            dma((4, half)),
            dma((4, half)),
            dma((4,)),
            dma((2,)),
            dma((2, half)),
            dma((4,)),
            dma((4,)),
            dma((2,)),
            dma((2,)),
            dma((2,)),
            dma((2,)),
        ],
        compiler_params=pltpu.CompilerParams(
            collective_id=0, has_side_effects=True, vmem_limit_bytes=48 * 1024 * 1024
        ),
    )(
        anomalies,
        innovations,
        sort_order.reshape(blocks, SORT),
        obs_error.reshape(blocks, SORT),
    )


def on_device(n, anomalies, innovations, sort_order, obs_error):
    rows, total = anomalies.shape
    if n % 4 or rows % 16 or (total // n) % (2 * TILE) or (rows * n) % TILE:
        return plain_on_device(anomalies, innovations, sort_order, obs_error)
    return fused_on_device(n, anomalies, innovations, sort_order, obs_error)


def solution(mesh):
    return jax.shard_map(
        functools.partial(on_device, mesh.shape["obs"]),
        mesh=mesh,
        in_specs=(
            P(("grp", "obs"), None),
            P(("grp", "obs"), None),
            P(("grp", "obs")),
            P(("grp", "obs")),
        ),
        out_specs=P(("grp", "obs"), None),
        check_vma=False,
    )
```

```python
import functools

import jax
import jax.numpy as jnp
from jax import lax
from jax.experimental import pallas as pl
from jax.experimental.pallas import tpu as pltpu
from jax.sharding import PartitionSpec as P


def shifted(shard, axis, by):
    peers = lax.axis_size(axis)
    pairs = [(i, i + by) for i in range(peers) if 0 <= i + by < peers]
    return lax.ppermute(shard, axis, pairs)


def gaspari(z):
    inner = z * z * (z * (z * (-0.25 * z + 0.5) + 0.625) - 5.0 / 3.0) + 1.0
    zs = jnp.maximum(z, 1.0)
    outer = (
        zs * zs * (zs * (zs * (zs / 12.0 - 0.5) + 0.625) + 5.0 / 3.0)
        - 5.0 * zs
        + 4.0
        - 2.0 / (3.0 * zs)
    )
    return jnp.where(z <= 1.0, inner, jnp.where(z < 2.0, outer, 0.0 * z))


def taper_scale(first_row, rows, cols, offset, half_width, members):
    row_ids = first_row + lax.iota(jnp.int32, rows)
    col_ids = lax.iota(jnp.int32, cols) + offset * cols
    dist = jnp.abs(row_ids[:, None] - col_ids[None, :]).astype(jnp.float32)
    return gaspari(dist / half_width) / (members - 1.0)


def permute_blocks(values, selector, width, blocks):
    shaped = values.reshape(values.shape[0], blocks, width)
    moved = jnp.einsum("mbi,bij->mbj", shaped, selector, preferred_element_type=jnp.float32)
    return moved.astype(jnp.bfloat16).reshape(values.shape[0], blocks * width)


def plain_on_device(anomalies, innovations, sort_order, obs_error):
    raw_y, raw_d = (
        lax.all_to_all(anomalies, "obs", split_axis=1, concat_axis=0, tiled=True),
        lax.all_to_all(innovations, "obs", split_axis=1, concat_axis=0, tiled=True),
    )
    members = raw_y.shape[0]
    panel = raw_y.shape[1]
    width = min(128, panel)
    blocks = panel // width
    local_ids = (sort_order % width).reshape(blocks, width)
    selector = (lax.iota(jnp.int32, width)[None, :, None] == local_ids[:, None, :]).astype(
        jnp.bfloat16
    )
    y_here = permute_blocks(raw_y, selector, width, blocks)
    d_here = permute_blocks(raw_d, selector, width, blocks)
    block = min(512, panel)
    half_width = panel // 2 * 1.0

    def tile_rows(first, y_cols, offset):
        row_part = lax.slice_in_dim(y_here, first, first + block, axis=1)
        gram = lax.dot_general(
            row_part, y_cols, (((0,), (0,)), ((), ())), preferred_element_type=jnp.float32
        )
        return (gram * taper_scale(first, block, panel, offset, half_width, members * 1.0)).astype(
            jnp.bfloat16
        )

    def apply_rows(weights, d_cols):
        return lax.dot_general(
            weights, d_cols, (((1,), (1,)), ((), ())), preferred_element_type=jnp.float32
        )

    pieces = []
    low_y, low_d = shifted((y_here, d_here), "obs", 1)
    up_y, up_d = shifted((y_here, d_here), "obs", -1)
    for first in range(0, panel, block):
        acc = apply_rows(tile_rows(first, y_here, 0), d_here)
        acc = acc + apply_rows(tile_rows(first, low_y, -1), low_d)
        acc = acc + apply_rows(tile_rows(first, up_y, 1), up_d)
        pieces.append(acc)
    total = jnp.concatenate(pieces, axis=0)
    return total + obs_error[:, None] * d_here.T.astype(jnp.float32)


TILE = 256
SORT = 128
MESH = pl.DeviceIdType.MESH
NT = (((1,), (1,)), ((), ()))
NN = (((1,), (0,)), ((), ()))


def mm(a, b, dims=NN):
    return lax.dot_general(a, b, dims, preferred_element_type=jnp.float32)


def kernel(
    n,
    y_hbm, d_hbm, order_hbm, err_hbm, out_ref,
    raw, y_ext, d_ext, y_t, weights, table, orders, errs, sel, sel_t, err_col,
    send_sem, recv_sem, own_sem, far_send, far_recv, swap_send, swap_recv,
    mate_send, mate_recv, order_sem, small_sem,
):
    me = lax.axis_index("obs")
    rows = y_hbm.shape[0]
    panel = y_hbm.shape[1] // n
    members = rows * n
    tiles = panel // TILE
    half = n // 2
    odd, side = me % 2, (me // 2) % 2
    mine = (me // 4) * 2 + odd
    own_slot = 1 - odd
    partner = me + 2 * odd - 1
    mate = me + 1 - 2 * odd
    has_low, has_up = me > 0, me < n - 1
    has_partner = (me > 0) & (me < n - 1)
    no_partner = (me == 0) | (me == n - 1)
    chunks = [(0, 0), (0, 1), (1, 0), (1, 1)]

    def here(slot):
        return has_low if slot == 0 else has_up

    def device_at(which, j):
        return (j // 2) * 4 + which * 2 + j % 2

    barrier = pltpu.get_barrier_semaphore()
    for k in range(1, n):
        pl.semaphore_signal(
            barrier, inc=1, device_id={"obs": lax.rem(me + k, n)}, device_id_type=MESH
        )
    pl.semaphore_wait(barrier, n - 1)

    def pair_panel(owner, slot):
        return owner - 1 + owner % 2 + slot

    def columns(at):
        return pl.ds(pl.multiple_of(at * panel, TILE), panel)

    def landing(a, slot, source):
        return raw.at[a, source // 4, (source // 2) % 2, source % 2, :, columns(slot)]

    def side_copy(i, k, owner, source):
        a, slot = chunks[i]
        return pltpu.make_async_remote_copy(
            src_ref=(y_hbm, d_hbm)[a].at[:, columns(pair_panel(owner, slot))],
            dst_ref=landing(a, slot, source),
            send_sem=send_sem.at[i, k],
            recv_sem=recv_sem.at[i, k],
            device_id={"obs": owner},
            device_id_type=MESH,
        )

    def own_copy(i):
        a, slot = chunks[i]
        return pltpu.make_async_copy(
            (y_hbm, d_hbm)[a].at[:, columns(pair_panel(me, slot))],
            landing(a, slot, me),
            own_sem.at[i],
        )

    def far_copy(a, owner, source, j):
        return pltpu.make_async_remote_copy(
            src_ref=(y_hbm, d_hbm)[a].at[:, columns(owner)],
            dst_ref=landing(a, 1 - owner % 2, source),
            send_sem=far_send.at[a],
            recv_sem=far_recv.at[a, j],
            device_id={"obs": owner},
            device_id_type=MESH,
        )

    def swap_copy(i, which):
        a, slot = chunks[i]
        part = raw.at[a, :, which, :, :, columns(slot)]
        return pltpu.make_async_remote_copy(
            src_ref=part,
            dst_ref=part,
            send_sem=swap_send.at[i],
            recv_sem=swap_recv.at[i],
            device_id={"obs": partner},
            device_id_type=MESH,
        )

    def mate_copy(a, parity):
        ext = (y_ext, d_ext)[a]
        there = columns(2 * parity)
        if a == 0:
            src, dst = ext.at[:, pl.ds(panel, panel)], ext.at[:, there]
        else:
            src, dst = ext.at[pl.ds(panel, panel)], ext.at[there]
        return pltpu.make_async_remote_copy(
            src_ref=src,
            dst_ref=dst,
            send_sem=mate_send.at[a],
            recv_sem=mate_recv.at[a],
            device_id={"obs": mate},
            device_id_type=MESH,
        )

    def order_copy(slot):
        return pltpu.make_async_remote_copy(
            src_ref=order_hbm,
            dst_ref=orders.at[slot],
            send_sem=order_sem.at[0],
            recv_sem=order_sem.at[1],
            device_id={"obs": partner},
            device_id_type=MESH,
        )

    far_owner = (1 - side) * (n - 1)
    steps = [half // 2]
    for step in range(1, half // 2):
        steps += [half // 2 + step, half // 2 - step]

    order_here = pltpu.make_async_copy(order_hbm, orders.at[own_slot], small_sem.at[0])
    err_here = pltpu.make_async_copy(err_hbm, errs, small_sem.at[1])
    order_here.start()
    err_here.start()

    @pl.when(has_partner)
    def _():
        order_copy(own_slot).start()

    def for_targets(i, act):
        for k in steps:
            owner = device_at(side, lax.rem(mine + k, half))
            if chunks[i][1] == 0:
                @pl.when(owner > 0)
                def _():
                    act(side_copy(i, k, owner, me))
            else:
                @pl.when(owner < n - 1)
                def _():
                    act(side_copy(i, k, owner, me))

    def start_chunk(i):
        a, slot = chunks[i]
        for_targets(i, lambda copy: copy.start())

        @pl.when(here(slot))
        def _():
            own_copy(i).start()

        if slot == 1:
            far_copy(a, far_owner, me, mine).start()

    start_chunk(0)
    start_chunk(1)

    row_id = lax.broadcasted_iota(jnp.int32, (SORT, SORT), 0)
    col_id = lax.broadcasted_iota(jnp.int32, (SORT, SORT), 1)
    err_here.wait()
    for b in range(panel // SORT):
        err = jnp.broadcast_to(errs[b : b + 1, :], (SORT, SORT))
        column = jnp.sum(jnp.where(row_id == col_id, err, 0.0), axis=1, keepdims=True)
        err_col[b * SORT : (b + 1) * SORT, :] = jnp.broadcast_to(column, (SORT, SORT))
    order_here.wait()

    @pl.when(has_partner)
    def _():
        order_copy(1 - own_slot).wait_recv()

    for slot in range(2):
        @pl.when(here(slot))
        def _():
            for b in range(panel // SORT):
                ids = jnp.broadcast_to(orders[slot, b : b + 1, :] & (SORT - 1), (SORT, SORT))
                pick = (row_id == ids).astype(jnp.float32)
                sel[slot, b] = pick.astype(jnp.bfloat16)
                sel_t[slot, b] = pick.T.astype(jnp.bfloat16)

    def make_table():
        r = lax.broadcasted_iota(jnp.int32, (TILE, TILE), 0)
        s = lax.broadcasted_iota(jnp.int32, (TILE, TILE), 1)
        for j in range(2 * tiles + 1):
            dist = jnp.abs(s - r + (j - tiles) * TILE).astype(jnp.float32)
            table[:, j * TILE : (j + 1) * TILE] = gaspari(dist / (panel // 2 * 1.0)) / (
                members - 1.0
            )

    def make_weights(j):
        for t in range(tiles):
            at = j - t
            if 0 <= at <= 2 * tiles:
                cols = slice(at * TILE, (at + 1) * TILE)
                gram = mm(y_t[t * TILE : (t + 1) * TILE, :], y_ext[:, j * TILE : (j + 1) * TILE])
                weights[t, :, cols] = (gram * table[:, cols]).astype(jnp.bfloat16)

    def weights_of(first, last):
        for j in range(first, last):
            make_weights(j)

    def apply_weights(first, last):
        for t in range(tiles):
            lo, hi = max(first, t), min(last, t + 2 * tiles + 1)
            if lo < hi:
                term = mm(
                    weights[t, :, (lo - t) * TILE : (hi - t) * TILE],
                    d_ext[lo * TILE : hi * TILE, :],
                )
                rows_here = slice(t * TILE, (t + 1) * TILE)
                out_ref[rows_here, :] = out_ref[rows_here, :] + term

    def of_partner(act):
        @pl.when((odd == 1) & has_up)
        def _():
            act(2 * tiles, 3 * tiles)

        @pl.when((odd == 0) & has_low)
        def _():
            act(0, tiles)

    def of_mate(act):
        @pl.when(odd == 1)
        def _():
            act(0, tiles)

        @pl.when(odd == 0)
        def _():
            act(2 * tiles, 3 * tiles)

    def gather(i):
        a, slot = chunks[i]

        @pl.when(here(slot))
        def _():
            own_copy(i).wait()
            for k in steps:
                source = device_at(side, lax.rem(mine + half - k, half))
                side_copy(i, k, me, source).wait_recv()

        @pl.when(has_partner)
        def _():
            swap_copy(i, side).start()

    def sort_chunk(i):
        a, slot = chunks[i]

        @pl.when(has_partner)
        def _():
            swap_copy(i, 1 - side).wait_recv()

        @pl.when(no_partner & (own_slot == slot))
        def _():
            for j in range(half):
                far_copy(a, me, device_at(1 - side, j), j).wait_recv()

        @pl.when(here(slot))
        def _():
            for b in range(panel // SORT):
                at = slice(slot * panel + b * SORT, slot * panel + (b + 1) * SORT)
                block = raw[a, :, :, :, :, at].reshape(members, SORT)
                start = pl.multiple_of((odd + slot) * panel + b * SORT, SORT)
                if a == 0:
                    y_ext[:, pl.ds(start, SORT)] = mm(block, sel[slot, b]).astype(jnp.bfloat16)
                else:
                    d_ext[pl.ds(start, SORT), :] = mm(sel_t[slot, b], block, NT).astype(
                        jnp.bfloat16
                    )

        @pl.when(own_slot == slot)
        def _():
            mate_copy(a, odd).start()
            for b in range(panel // SORT):
                cols = slice(b * SORT, (b + 1) * SORT)
                if a == 0:
                    at = slice(slot * panel + b * SORT, slot * panel + (b + 1) * SORT)
                    block = raw[a, :, :, :, :, at].reshape(members, SORT)
                    y_t[cols, :] = mm(sel_t[slot, b], block, NT).astype(jnp.bfloat16)
                else:
                    own = d_ext[panel + b * SORT : panel + (b + 1) * SORT, :]
                    out_ref[cols, :] = err_col[cols, 0:1] * own.astype(jnp.float32)

    gather(0)
    start_chunk(2)
    make_table()
    gather(1)
    start_chunk(3)
    sort_chunk(0)
    gather(2)
    sort_chunk(1)
    weights_of(tiles, 2 * tiles)
    of_partner(weights_of)
    gather(3)
    mate_copy(0, 1 - odd).wait_recv()
    of_mate(weights_of)
    sort_chunk(2)
    sort_chunk(3)
    apply_weights(tiles, 2 * tiles)
    of_partner(apply_weights)
    mate_copy(1, 1 - odd).wait_recv()
    of_mate(apply_weights)

    for i, (a, slot) in enumerate(chunks):
        for_targets(i, lambda copy: copy.wait_send())
        if slot == 1:
            far_copy(a, far_owner, me, mine).wait_send()
            mate_copy(a, odd).wait_send()

        @pl.when(has_partner)
        def _():
            swap_copy(i, side).wait_send()

    @pl.when(has_partner)
    def _():
        order_copy(own_slot).wait_send()


def fused_on_device(n, anomalies, innovations, sort_order, obs_error):
    rows, total = anomalies.shape
    panel = total // n
    members = rows * n
    tiles = panel // TILE
    blocks = panel // SORT
    half = n // 2
    bf16, f32 = jnp.bfloat16, jnp.float32
    hbm = pl.BlockSpec(memory_space=pltpu.HBM)
    dma = pltpu.SemaphoreType.DMA
    return pl.pallas_call(
        functools.partial(kernel, n),
        out_shape=jax.ShapeDtypeStruct((panel, members), f32),
        in_specs=[hbm] * 4,
        out_specs=pl.BlockSpec(memory_space=pltpu.VMEM),
        scratch_shapes=[
            pltpu.VMEM((2, n // 4, 2, 2, rows, 2 * panel), bf16),
            pltpu.VMEM((members, 3 * panel), bf16),
            pltpu.VMEM((3 * panel, members), bf16),
            pltpu.VMEM((panel, members), bf16),
            pltpu.VMEM((tiles, TILE, (2 * tiles + 1) * TILE), bf16),
            pltpu.VMEM((TILE, (2 * tiles + 1) * TILE), f32),
            pltpu.VMEM((2, blocks, SORT), jnp.int32),
            pltpu.VMEM((blocks, SORT), f32),
            pltpu.VMEM((2, blocks, SORT, SORT), bf16),
            pltpu.VMEM((2, blocks, SORT, SORT), bf16),
            pltpu.VMEM((panel, SORT), f32),
            dma((4, half)),
            dma((4, half)),
            dma((4,)),
            dma((2,)),
            dma((2, half)),
            dma((4,)),
            dma((4,)),
            dma((2,)),
            dma((2,)),
            dma((2,)),
            dma((2,)),
        ],
        compiler_params=pltpu.CompilerParams(
            collective_id=0, has_side_effects=True, vmem_limit_bytes=63 * 1024 * 1024
        ),
    )(
        anomalies,
        innovations,
        sort_order.reshape(blocks, SORT),
        obs_error.reshape(blocks, SORT),
    )


def on_device(n, anomalies, innovations, sort_order, obs_error):
    rows, total = anomalies.shape
    if n % 4 or rows % 16 or (total // n) % (2 * TILE) or (rows * n) % TILE:
        return plain_on_device(anomalies, innovations, sort_order, obs_error)
    return fused_on_device(n, anomalies, innovations, sort_order, obs_error)


def solution(mesh):
    return jax.shard_map(
        functools.partial(on_device, mesh.shape["obs"]),
        mesh=mesh,
        in_specs=(
            P(("grp", "obs"), None),
            P(("grp", "obs"), None),
            P(("grp", "obs")),
            P(("grp", "obs")),
        ),
        out_specs=P(("grp", "obs"), None),
        check_vma=False,
    )
```

```python
import functools

import jax
import jax.numpy as jnp
from jax import lax
from jax.experimental import pallas as pl
from jax.experimental.pallas import tpu as pltpu
from jax.sharding import PartitionSpec as P


def shifted(shard, axis, by):
    peers = lax.axis_size(axis)
    pairs = [(i, i + by) for i in range(peers) if 0 <= i + by < peers]
    return lax.ppermute(shard, axis, pairs)


def gaspari(z):
    inner = z * z * (z * (z * (-0.25 * z + 0.5) + 0.625) - 5.0 / 3.0) + 1.0
    zs = jnp.maximum(z, 1.0)
    outer = (
        zs * zs * (zs * (zs * (zs / 12.0 - 0.5) + 0.625) + 5.0 / 3.0)
        - 5.0 * zs
        + 4.0
        - 2.0 / (3.0 * zs)
    )
    return jnp.where(z <= 1.0, inner, jnp.where(z < 2.0, outer, 0.0 * z))


def taper_scale(first_row, rows, cols, offset, half_width, members):
    row_ids = first_row + lax.iota(jnp.int32, rows)
    col_ids = lax.iota(jnp.int32, cols) + offset * cols
    dist = jnp.abs(row_ids[:, None] - col_ids[None, :]).astype(jnp.float32)
    return gaspari(dist / half_width) / (members - 1.0)


def permute_blocks(values, selector, width, blocks):
    shaped = values.reshape(values.shape[0], blocks, width)
    moved = jnp.einsum("mbi,bij->mbj", shaped, selector, preferred_element_type=jnp.float32)
    return moved.astype(jnp.bfloat16).reshape(values.shape[0], blocks * width)


def plain_on_device(anomalies, innovations, sort_order, obs_error):
    raw_y, raw_d = (
        lax.all_to_all(anomalies, "obs", split_axis=1, concat_axis=0, tiled=True),
        lax.all_to_all(innovations, "obs", split_axis=1, concat_axis=0, tiled=True),
    )
    members = raw_y.shape[0]
    panel = raw_y.shape[1]
    width = min(128, panel)
    blocks = panel // width
    local_ids = (sort_order % width).reshape(blocks, width)
    selector = (lax.iota(jnp.int32, width)[None, :, None] == local_ids[:, None, :]).astype(
        jnp.bfloat16
    )
    y_here = permute_blocks(raw_y, selector, width, blocks)
    d_here = permute_blocks(raw_d, selector, width, blocks)
    block = min(512, panel)
    half_width = panel // 2 * 1.0

    def tile_rows(first, y_cols, offset):
        row_part = lax.slice_in_dim(y_here, first, first + block, axis=1)
        gram = lax.dot_general(
            row_part, y_cols, (((0,), (0,)), ((), ())), preferred_element_type=jnp.float32
        )
        return (gram * taper_scale(first, block, panel, offset, half_width, members * 1.0)).astype(
            jnp.bfloat16
        )

    def apply_rows(weights, d_cols):
        return lax.dot_general(
            weights, d_cols, (((1,), (1,)), ((), ())), preferred_element_type=jnp.float32
        )

    pieces = []
    low_y, low_d = shifted((y_here, d_here), "obs", 1)
    up_y, up_d = shifted((y_here, d_here), "obs", -1)
    for first in range(0, panel, block):
        acc = apply_rows(tile_rows(first, y_here, 0), d_here)
        acc = acc + apply_rows(tile_rows(first, low_y, -1), low_d)
        acc = acc + apply_rows(tile_rows(first, up_y, 1), up_d)
        pieces.append(acc)
    total = jnp.concatenate(pieces, axis=0)
    return total + obs_error[:, None] * d_here.T.astype(jnp.float32)


TILE = 256
SORT = 128
MESH = pl.DeviceIdType.MESH
NT = (((1,), (1,)), ((), ()))
NN = (((1,), (0,)), ((), ()))


def mm(a, b, dims=NN):
    return lax.dot_general(a, b, dims, preferred_element_type=jnp.float32)


def kernel(
    n,
    y_hbm, d_hbm, order_hbm, err_hbm, out_ref,
    raw, y_ext, d_ext, y_t, weights, table, orders, errs, sel, sel_t, err_col,
    send_sem, recv_sem, own_sem, far_send, far_recv, swap_send, swap_recv,
    mate_send, mate_recv, order_sem, small_sem,
):
    me = lax.axis_index("obs")
    rows = y_hbm.shape[0]
    panel = y_hbm.shape[1] // n
    members = rows * n
    tiles = panel // TILE
    half = n // 2
    odd, side = me % 2, (me // 2) % 2
    mine = (me // 4) * 2 + odd
    own_slot = 1 - odd
    partner = me + 2 * odd - 1
    mate = me + 1 - 2 * odd
    has_low, has_up = me > 0, me < n - 1
    has_partner = (me > 0) & (me < n - 1)
    no_partner = (me == 0) | (me == n - 1)
    part = panel // 2
    chunks = [(0, 0, 0, panel), (0, 1, 0, panel)] + [
        (1, slot, first, part) for first in (0, part) for slot in range(2)
    ]

    def here(slot):
        return has_low if slot == 0 else has_up

    def device_at(which, j):
        return (j // 2) * 4 + which * 2 + j % 2

    barrier = pltpu.get_barrier_semaphore()
    for k in range(1, n):
        pl.semaphore_signal(
            barrier, inc=1, device_id={"obs": lax.rem(me + k, n)}, device_id_type=MESH
        )
    pl.semaphore_wait(barrier, n - 1)

    def pair_panel(owner, slot):
        return owner - 1 + owner % 2 + slot

    def columns(at, first=0, width=panel):
        return pl.ds(pl.multiple_of(at * panel + first, TILE), width)

    def landing(a, slot, source, first=0, width=panel):
        at = columns(slot, first, width)
        return raw.at[a, source // 4, (source // 2) % 2, source % 2, :, at]

    def side_copy(i, k, owner, source):
        a, slot, first, width = chunks[i]
        return pltpu.make_async_remote_copy(
            src_ref=(y_hbm, d_hbm)[a].at[:, columns(pair_panel(owner, slot), first, width)],
            dst_ref=landing(a, slot, source, first, width),
            send_sem=send_sem.at[i, k],
            recv_sem=recv_sem.at[i, k],
            device_id={"obs": owner},
            device_id_type=MESH,
        )

    def own_copy(i):
        a, slot, first, width = chunks[i]
        return pltpu.make_async_copy(
            (y_hbm, d_hbm)[a].at[:, columns(pair_panel(me, slot), first, width)],
            landing(a, slot, me, first, width),
            own_sem.at[i],
        )

    def far_copy(a, owner, source, j):
        return pltpu.make_async_remote_copy(
            src_ref=(y_hbm, d_hbm)[a].at[:, columns(owner)],
            dst_ref=landing(a, 1 - owner % 2, source),
            send_sem=far_send.at[a],
            recv_sem=far_recv.at[a, j],
            device_id={"obs": owner},
            device_id_type=MESH,
        )

    def swap_copy(i, which):
        a, slot, first, width = chunks[i]
        held = raw.at[a, :, which, :, :, columns(slot, first, width)]
        return pltpu.make_async_remote_copy(
            src_ref=held,
            dst_ref=held,
            send_sem=swap_send.at[i],
            recv_sem=swap_recv.at[i],
            device_id={"obs": partner},
            device_id_type=MESH,
        )

    def mate_copy(a, parity, first=0, width=panel):
        ext = (y_ext, d_ext)[a]
        there = columns(2 * parity, first, width)
        if a == 0:
            src, dst = ext.at[:, pl.ds(panel, panel)], ext.at[:, there]
        else:
            src, dst = ext.at[pl.ds(panel + first, width)], ext.at[there]
        return pltpu.make_async_remote_copy(
            src_ref=src,
            dst_ref=dst,
            send_sem=mate_send.at[a, first // part],
            recv_sem=mate_recv.at[a, first // part],
            device_id={"obs": mate},
            device_id_type=MESH,
        )

    def order_copy(slot):
        return pltpu.make_async_remote_copy(
            src_ref=order_hbm,
            dst_ref=orders.at[slot],
            send_sem=order_sem.at[0],
            recv_sem=order_sem.at[1],
            device_id={"obs": partner},
            device_id_type=MESH,
        )

    far_owner = (1 - side) * (n - 1)
    steps = [half // 2]
    for step in range(1, half // 2):
        steps += [half // 2 + step, half // 2 - step]

    order_here = pltpu.make_async_copy(order_hbm, orders.at[own_slot], small_sem.at[0])
    err_here = pltpu.make_async_copy(err_hbm, errs, small_sem.at[1])
    order_here.start()
    err_here.start()

    @pl.when(has_partner)
    def _():
        order_copy(own_slot).start()

    def for_targets(i, act):
        for k in steps:
            owner = device_at(side, lax.rem(mine + k, half))
            if chunks[i][1] == 0:
                @pl.when(owner > 0)
                def _():
                    act(side_copy(i, k, owner, me))
            else:
                @pl.when(owner < n - 1)
                def _():
                    act(side_copy(i, k, owner, me))

    def start_chunk(i):
        a, slot, first, width = chunks[i]
        for_targets(i, lambda copy: copy.start())

        @pl.when(here(slot))
        def _():
            own_copy(i).start()

        if slot == 1 and first == 0:
            far_copy(a, far_owner, me, mine).start()

    start_chunk(0)
    start_chunk(1)
    start_chunk(2)

    row_id = lax.broadcasted_iota(jnp.int32, (SORT, SORT), 0)
    col_id = lax.broadcasted_iota(jnp.int32, (SORT, SORT), 1)
    err_here.wait()
    for b in range(panel // SORT):
        err = jnp.broadcast_to(errs[b : b + 1, :], (SORT, SORT))
        column = jnp.sum(jnp.where(row_id == col_id, err, 0.0), axis=1, keepdims=True)
        err_col[b * SORT : (b + 1) * SORT, :] = jnp.broadcast_to(column, (SORT, SORT))
    order_here.wait()

    @pl.when(has_partner)
    def _():
        order_copy(1 - own_slot).wait_recv()

    for slot in range(2):
        @pl.when(here(slot))
        def _():
            for b in range(panel // SORT):
                ids = jnp.broadcast_to(orders[slot, b : b + 1, :] & (SORT - 1), (SORT, SORT))
                pick = (row_id == ids).astype(jnp.float32)
                sel[slot, b] = pick.astype(jnp.bfloat16)
                sel_t[slot, b] = pick.T.astype(jnp.bfloat16)

    def make_table():
        r = lax.broadcasted_iota(jnp.int32, (TILE, TILE), 0)
        s = lax.broadcasted_iota(jnp.int32, (TILE, TILE), 1)
        for j in range(2 * tiles + 1):
            dist = jnp.abs(s - r + (j - tiles) * TILE).astype(jnp.float32)
            table[:, j * TILE : (j + 1) * TILE] = gaspari(dist / (panel // 2 * 1.0)) / (
                members - 1.0
            )

    def make_weights(j):
        for t in range(tiles):
            at = j - t
            if 0 <= at <= 2 * tiles:
                cols = slice(at * TILE, (at + 1) * TILE)
                gram = mm(y_t[t * TILE : (t + 1) * TILE, :], y_ext[:, j * TILE : (j + 1) * TILE])
                weights[t, :, cols] = (gram * table[:, cols]).astype(jnp.bfloat16)

    def weights_of(first, last):
        for j in range(first, last):
            make_weights(j)

    def apply_weights(first, last):
        for t in range(tiles):
            lo, hi = max(first, t), min(last, t + 2 * tiles + 1)
            if lo < hi:
                term = mm(
                    weights[t, :, (lo - t) * TILE : (hi - t) * TILE],
                    d_ext[lo * TILE : hi * TILE, :],
                )
                rows_here = slice(t * TILE, (t + 1) * TILE)
                out_ref[rows_here, :] = out_ref[rows_here, :] + term

    def of_partner(act):
        @pl.when((odd == 1) & has_up)
        def _():
            act(2 * tiles, 3 * tiles)

        @pl.when((odd == 0) & has_low)
        def _():
            act(0, tiles)

    def of_mate(act):
        @pl.when(odd == 1)
        def _():
            act(0, tiles)

        @pl.when(odd == 0)
        def _():
            act(2 * tiles, 3 * tiles)

    def gather(i):
        a, slot, first, width = chunks[i]

        @pl.when(here(slot))
        def _():
            own_copy(i).wait()
            for k in steps:
                source = device_at(side, lax.rem(mine + half - k, half))
                side_copy(i, k, me, source).wait_recv()

        @pl.when(has_partner)
        def _():
            swap_copy(i, side).start()

    def sort_chunk(i):
        a, slot, first, width = chunks[i]

        @pl.when(has_partner)
        def _():
            swap_copy(i, 1 - side).wait_recv()

        @pl.when(no_partner & (own_slot == slot))
        def _():
            if first == 0:
                for j in range(half):
                    far_copy(a, me, device_at(1 - side, j), j).wait_recv()

        @pl.when(here(slot))
        def _():
            for b in range(first // SORT, (first + width) // SORT):
                at = slice(slot * panel + b * SORT, slot * panel + (b + 1) * SORT)
                block = raw[a, :, :, :, :, at].reshape(members, SORT)
                start = pl.multiple_of((odd + slot) * panel + b * SORT, SORT)
                if a == 0:
                    y_ext[:, pl.ds(start, SORT)] = mm(block, sel[slot, b]).astype(jnp.bfloat16)
                else:
                    d_ext[pl.ds(start, SORT), :] = mm(sel_t[slot, b], block, NT).astype(
                        jnp.bfloat16
                    )

        @pl.when(own_slot == slot)
        def _():
            mate_copy(a, odd, first, width).start()
            for b in range(first // SORT, (first + width) // SORT):
                cols = slice(b * SORT, (b + 1) * SORT)
                if a == 0:
                    at = slice(slot * panel + b * SORT, slot * panel + (b + 1) * SORT)
                    block = raw[a, :, :, :, :, at].reshape(members, SORT)
                    y_t[cols, :] = mm(sel_t[slot, b], block, NT).astype(jnp.bfloat16)
                else:
                    own = d_ext[panel + b * SORT : panel + (b + 1) * SORT, :]
                    out_ref[cols, :] = err_col[cols, 0:1] * own.astype(jnp.float32)

    gather(0)
    start_chunk(3)
    make_table()
    gather(1)
    start_chunk(4)
    sort_chunk(0)
    gather(2)
    start_chunk(5)
    sort_chunk(1)
    weights_of(tiles, 2 * tiles)
    gather(3)
    of_partner(weights_of)
    gather(4)
    mate_copy(0, 1 - odd).wait_recv()
    of_mate(weights_of)
    gather(5)
    for i in range(2, 6):
        sort_chunk(i)
    apply_weights(tiles, 2 * tiles)
    of_partner(apply_weights)
    for first in (0, part):
        mate_copy(1, 1 - odd, first, part).wait_recv()
    of_mate(apply_weights)

    for i, (a, slot, first, width) in enumerate(chunks):
        for_targets(i, lambda copy: copy.wait_send())
        if slot == 1:
            mate_copy(a, odd, first, width).wait_send()
            if first == 0:
                far_copy(a, far_owner, me, mine).wait_send()

        @pl.when(has_partner)
        def _():
            swap_copy(i, side).wait_send()

    @pl.when(has_partner)
    def _():
        order_copy(own_slot).wait_send()


def fused_on_device(n, anomalies, innovations, sort_order, obs_error):
    rows, total = anomalies.shape
    panel = total // n
    members = rows * n
    tiles = panel // TILE
    blocks = panel // SORT
    half = n // 2
    bf16, f32 = jnp.bfloat16, jnp.float32
    hbm = pl.BlockSpec(memory_space=pltpu.HBM)
    dma = pltpu.SemaphoreType.DMA
    return pl.pallas_call(
        functools.partial(kernel, n),
        out_shape=jax.ShapeDtypeStruct((panel, members), f32),
        in_specs=[hbm] * 4,
        out_specs=pl.BlockSpec(memory_space=pltpu.VMEM),
        scratch_shapes=[
            pltpu.VMEM((2, n // 4, 2, 2, rows, 2 * panel), bf16),
            pltpu.VMEM((members, 3 * panel), bf16),
            pltpu.VMEM((3 * panel, members), bf16),
            pltpu.VMEM((panel, members), bf16),
            pltpu.VMEM((tiles, TILE, (2 * tiles + 1) * TILE), bf16),
            pltpu.VMEM((TILE, (2 * tiles + 1) * TILE), f32),
            pltpu.VMEM((2, blocks, SORT), jnp.int32),
            pltpu.VMEM((blocks, SORT), f32),
            pltpu.VMEM((2, blocks, SORT, SORT), bf16),
            pltpu.VMEM((2, blocks, SORT, SORT), bf16),
            pltpu.VMEM((panel, SORT), f32),
            dma((6, half)),
            dma((6, half)),
            dma((6,)),
            dma((2,)),
            dma((2, half)),
            dma((6,)),
            dma((6,)),
            dma((2, 2)),
            dma((2, 2)),
            dma((2,)),
            dma((2,)),
        ],
        compiler_params=pltpu.CompilerParams(
            collective_id=0, has_side_effects=True, vmem_limit_bytes=64512 * 1024
        ),
    )(
        anomalies,
        innovations,
        sort_order.reshape(blocks, SORT),
        obs_error.reshape(blocks, SORT),
    )


def on_device(n, anomalies, innovations, sort_order, obs_error):
    rows, total = anomalies.shape
    if n % 4 or rows % 16 or (total // n) % (2 * TILE) or (rows * n) % TILE:
        return plain_on_device(anomalies, innovations, sort_order, obs_error)
    return fused_on_device(n, anomalies, innovations, sort_order, obs_error)


def solution(mesh):
    return jax.shard_map(
        functools.partial(on_device, mesh.shape["obs"]),
        mesh=mesh,
        in_specs=(
            P(("grp", "obs"), None),
            P(("grp", "obs"), None),
            P(("grp", "obs")),
            P(("grp", "obs")),
        ),
        out_specs=P(("grp", "obs"), None),
        check_vma=False,
    )
```

```python
import functools

import jax
import jax.numpy as jnp
from jax import lax
from jax.experimental import pallas as pl
from jax.experimental.pallas import tpu as pltpu
from jax.sharding import PartitionSpec as P


def shifted(shard, axis, by):
    peers = lax.axis_size(axis)
    pairs = [(i, i + by) for i in range(peers) if 0 <= i + by < peers]
    return lax.ppermute(shard, axis, pairs)


def gaspari(z):
    inner = z * z * (z * (z * (-0.25 * z + 0.5) + 0.625) - 5.0 / 3.0) + 1.0
    zs = jnp.maximum(z, 1.0)
    outer = (
        zs * zs * (zs * (zs * (zs / 12.0 - 0.5) + 0.625) + 5.0 / 3.0)
        - 5.0 * zs
        + 4.0
        - 2.0 / (3.0 * zs)
    )
    return jnp.where(z <= 1.0, inner, jnp.where(z < 2.0, outer, 0.0 * z))


def taper_scale(first_row, rows, cols, offset, half_width, members):
    row_ids = first_row + lax.iota(jnp.int32, rows)
    col_ids = lax.iota(jnp.int32, cols) + offset * cols
    dist = jnp.abs(row_ids[:, None] - col_ids[None, :]).astype(jnp.float32)
    return gaspari(dist / half_width) / (members - 1.0)


def permute_blocks(values, selector, width, blocks):
    shaped = values.reshape(values.shape[0], blocks, width)
    moved = jnp.einsum("mbi,bij->mbj", shaped, selector, preferred_element_type=jnp.float32)
    return moved.astype(jnp.bfloat16).reshape(values.shape[0], blocks * width)


def plain_on_device(anomalies, innovations, sort_order, obs_error):
    raw_y, raw_d = (
        lax.all_to_all(anomalies, "obs", split_axis=1, concat_axis=0, tiled=True),
        lax.all_to_all(innovations, "obs", split_axis=1, concat_axis=0, tiled=True),
    )
    members = raw_y.shape[0]
    panel = raw_y.shape[1]
    width = min(128, panel)
    blocks = panel // width
    local_ids = (sort_order % width).reshape(blocks, width)
    selector = (lax.iota(jnp.int32, width)[None, :, None] == local_ids[:, None, :]).astype(
        jnp.bfloat16
    )
    y_here = permute_blocks(raw_y, selector, width, blocks)
    d_here = permute_blocks(raw_d, selector, width, blocks)
    block = min(512, panel)
    half_width = panel // 2 * 1.0

    def tile_rows(first, y_cols, offset):
        row_part = lax.slice_in_dim(y_here, first, first + block, axis=1)
        gram = lax.dot_general(
            row_part, y_cols, (((0,), (0,)), ((), ())), preferred_element_type=jnp.float32
        )
        return (gram * taper_scale(first, block, panel, offset, half_width, members * 1.0)).astype(
            jnp.bfloat16
        )

    def apply_rows(weights, d_cols):
        return lax.dot_general(
            weights, d_cols, (((1,), (1,)), ((), ())), preferred_element_type=jnp.float32
        )

    pieces = []
    low_y, low_d = shifted((y_here, d_here), "obs", 1)
    up_y, up_d = shifted((y_here, d_here), "obs", -1)
    for first in range(0, panel, block):
        acc = apply_rows(tile_rows(first, y_here, 0), d_here)
        acc = acc + apply_rows(tile_rows(first, low_y, -1), low_d)
        acc = acc + apply_rows(tile_rows(first, up_y, 1), up_d)
        pieces.append(acc)
    total = jnp.concatenate(pieces, axis=0)
    return total + obs_error[:, None] * d_here.T.astype(jnp.float32)


TILE = 256
SORT = 128
MESH = pl.DeviceIdType.MESH
NT = (((1,), (1,)), ((), ()))
NN = (((1,), (0,)), ((), ()))


def mm(a, b, dims=NN):
    return lax.dot_general(a, b, dims, preferred_element_type=jnp.float32)


def kernel(
    n,
    y_hbm, d_hbm, order_hbm, err_hbm, out_ref,
    raw, y_ext, d_ext, y_t, weights, table, orders, errs, sel, sel_t, err_col,
    send_sem, recv_sem, own_sem, far_send, far_recv, swap_send, swap_recv,
    mate_send, mate_recv, order_sem, small_sem,
):
    me = lax.axis_index("obs")
    rows = y_hbm.shape[0]
    panel = y_hbm.shape[1] // n
    members = rows * n
    tiles = panel // TILE
    half = n // 2
    odd, side = me % 2, (me // 2) % 2
    mine = (me // 4) * 2 + odd
    own_slot = 1 - odd
    partner = me + 2 * odd - 1
    mate = me + 1 - 2 * odd
    has_low, has_up = me > 0, me < n - 1
    has_partner = (me > 0) & (me < n - 1)
    no_partner = (me == 0) | (me == n - 1)
    chunks = [(0, 0), (0, 1), (1, 0), (1, 1)]

    def here(slot):
        return has_low if slot == 0 else has_up

    def device_at(which, j):
        return (j // 2) * 4 + which * 2 + j % 2

    barrier = pltpu.get_barrier_semaphore()
    for k in range(1, n):
        pl.semaphore_signal(
            barrier, inc=1, device_id={"obs": lax.rem(me + k, n)}, device_id_type=MESH
        )
    pl.semaphore_wait(barrier, n - 1)

    def pair_panel(owner, slot):
        return owner - 1 + owner % 2 + slot

    def columns(at):
        return pl.ds(pl.multiple_of(at * panel, TILE), panel)

    def landing(a, slot, source):
        return raw.at[a, source // 4, (source // 2) % 2, source % 2, :, columns(slot)]

    def side_copy(i, k, owner, source):
        a, slot = chunks[i]
        return pltpu.make_async_remote_copy(
            src_ref=(y_hbm, d_hbm)[a].at[:, columns(pair_panel(owner, slot))],
            dst_ref=landing(a, slot, source),
            send_sem=send_sem.at[i, k],
            recv_sem=recv_sem.at[i, k],
            device_id={"obs": owner},
            device_id_type=MESH,
        )

    def own_copy(i):
        a, slot = chunks[i]
        return pltpu.make_async_copy(
            (y_hbm, d_hbm)[a].at[:, columns(pair_panel(me, slot))],
            landing(a, slot, me),
            own_sem.at[i],
        )

    def far_copy(a, owner, source, j):
        return pltpu.make_async_remote_copy(
            src_ref=(y_hbm, d_hbm)[a].at[:, columns(owner)],
            dst_ref=landing(a, 1 - owner % 2, source),
            send_sem=far_send.at[a],
            recv_sem=far_recv.at[a, j],
            device_id={"obs": owner},
            device_id_type=MESH,
        )

    def swap_copy(i, which):
        a, slot = chunks[i]
        part = raw.at[a, :, which, :, :, columns(slot)]
        return pltpu.make_async_remote_copy(
            src_ref=part,
            dst_ref=part,
            send_sem=swap_send.at[i],
            recv_sem=swap_recv.at[i],
            device_id={"obs": partner},
            device_id_type=MESH,
        )

    def mate_copy(a, parity):
        ext = (y_ext, d_ext)[a]
        there = columns(2 * parity)
        if a == 0:
            src, dst = ext.at[:, pl.ds(panel, panel)], ext.at[:, there]
        else:
            src, dst = ext.at[pl.ds(panel, panel)], ext.at[there]
        return pltpu.make_async_remote_copy(
            src_ref=src,
            dst_ref=dst,
            send_sem=mate_send.at[a],
            recv_sem=mate_recv.at[a],
            device_id={"obs": mate},
            device_id_type=MESH,
        )

    def order_copy(slot):
        return pltpu.make_async_remote_copy(
            src_ref=order_hbm,
            dst_ref=orders.at[slot],
            send_sem=order_sem.at[0],
            recv_sem=order_sem.at[1],
            device_id={"obs": partner},
            device_id_type=MESH,
        )

    far_owner = (1 - side) * (n - 1)
    steps = [half // 2]
    for step in range(1, half // 2):
        steps += [half // 2 + step, half // 2 - step]

    order_here = pltpu.make_async_copy(order_hbm, orders.at[own_slot], small_sem.at[0])
    err_here = pltpu.make_async_copy(err_hbm, errs, small_sem.at[1])
    order_here.start()
    err_here.start()

    @pl.when(has_partner)
    def _():
        order_copy(own_slot).start()

    def for_targets(i, act):
        for k in steps:
            owner = device_at(side, lax.rem(mine + k, half))
            if chunks[i][1] == 0:
                @pl.when(owner > 0)
                def _():
                    act(side_copy(i, k, owner, me))
            else:
                @pl.when(owner < n - 1)
                def _():
                    act(side_copy(i, k, owner, me))

    def start_chunk(i):
        a, slot = chunks[i]
        for_targets(i, lambda copy: copy.start())

        @pl.when(here(slot))
        def _():
            own_copy(i).start()

        if slot == 1:
            far_copy(a, far_owner, me, mine).start()

    start_chunk(0)
    start_chunk(1)
    start_chunk(2)

    row_id = lax.broadcasted_iota(jnp.int32, (SORT, SORT), 0)
    col_id = lax.broadcasted_iota(jnp.int32, (SORT, SORT), 1)
    err_here.wait()
    for b in range(panel // SORT):
        err = jnp.broadcast_to(errs[b : b + 1, :], (SORT, SORT))
        column = jnp.sum(jnp.where(row_id == col_id, err, 0.0), axis=1, keepdims=True)
        err_col[b * SORT : (b + 1) * SORT, :] = jnp.broadcast_to(column, (SORT, SORT))
    order_here.wait()

    @pl.when(has_partner)
    def _():
        order_copy(1 - own_slot).wait_recv()

    for slot in range(2):
        @pl.when(here(slot))
        def _():
            for b in range(panel // SORT):
                ids = jnp.broadcast_to(orders[slot, b : b + 1, :] & (SORT - 1), (SORT, SORT))
                pick = (row_id == ids).astype(jnp.float32)
                sel[slot, b] = pick.astype(jnp.bfloat16)
                sel_t[slot, b] = pick.T.astype(jnp.bfloat16)

    def make_table():
        r = lax.broadcasted_iota(jnp.int32, (TILE, TILE), 0)
        s = lax.broadcasted_iota(jnp.int32, (TILE, TILE), 1)
        for j in range(2 * tiles + 1):
            dist = jnp.abs(s - r + (j - tiles) * TILE).astype(jnp.float32)
            table[:, j * TILE : (j + 1) * TILE] = gaspari(dist / (panel // 2 * 1.0)) / (
                members - 1.0
            )

    def make_weights(j):
        for t in range(tiles):
            at = j - t
            if 0 <= at <= 2 * tiles:
                cols = slice(at * TILE, (at + 1) * TILE)
                gram = mm(y_t[t * TILE : (t + 1) * TILE, :], y_ext[:, j * TILE : (j + 1) * TILE])
                weights[t, :, cols] = (gram * table[:, cols]).astype(jnp.bfloat16)

    def weights_of(first, last):
        for j in range(first, last):
            make_weights(j)

    def apply_weights(first, last):
        for t in range(tiles):
            lo, hi = max(first, t), min(last, t + 2 * tiles + 1)
            if lo < hi:
                term = mm(
                    weights[t, :, (lo - t) * TILE : (hi - t) * TILE],
                    d_ext[lo * TILE : hi * TILE, :],
                )
                rows_here = slice(t * TILE, (t + 1) * TILE)
                out_ref[rows_here, :] = out_ref[rows_here, :] + term

    def of_partner(act):
        @pl.when((odd == 1) & has_up)
        def _():
            act(2 * tiles, 3 * tiles)

        @pl.when((odd == 0) & has_low)
        def _():
            act(0, tiles)

    def of_mate(act):
        @pl.when(odd == 1)
        def _():
            act(0, tiles)

        @pl.when(odd == 0)
        def _():
            act(2 * tiles, 3 * tiles)

    def gather(i):
        a, slot = chunks[i]

        @pl.when(here(slot))
        def _():
            own_copy(i).wait()
            for k in steps:
                source = device_at(side, lax.rem(mine + half - k, half))
                side_copy(i, k, me, source).wait_recv()

        @pl.when(has_partner)
        def _():
            swap_copy(i, side).start()

    def sort_chunk(i):
        a, slot = chunks[i]

        @pl.when(has_partner)
        def _():
            swap_copy(i, 1 - side).wait_recv()

        @pl.when(no_partner & (own_slot == slot))
        def _():
            for j in range(half):
                far_copy(a, me, device_at(1 - side, j), j).wait_recv()

        @pl.when(here(slot))
        def _():
            for b in range(panel // SORT):
                at = slice(slot * panel + b * SORT, slot * panel + (b + 1) * SORT)
                block = raw[a, :, :, :, :, at].reshape(members, SORT)
                start = pl.multiple_of((odd + slot) * panel + b * SORT, SORT)
                if a == 0:
                    y_ext[:, pl.ds(start, SORT)] = mm(block, sel[slot, b]).astype(jnp.bfloat16)
                else:
                    d_ext[pl.ds(start, SORT), :] = mm(sel_t[slot, b], block, NT).astype(
                        jnp.bfloat16
                    )

        @pl.when(own_slot == slot)
        def _():
            mate_copy(a, odd).start()
            for b in range(panel // SORT):
                cols = slice(b * SORT, (b + 1) * SORT)
                if a == 0:
                    at = slice(slot * panel + b * SORT, slot * panel + (b + 1) * SORT)
                    block = raw[a, :, :, :, :, at].reshape(members, SORT)
                    y_t[cols, :] = mm(sel_t[slot, b], block, NT).astype(jnp.bfloat16)
                else:
                    own = d_ext[panel + b * SORT : panel + (b + 1) * SORT, :]
                    out_ref[cols, :] = err_col[cols, 0:1] * own.astype(jnp.float32)

    gather(0)
    start_chunk(3)
    make_table()
    gather(1)
    sort_chunk(0)
    gather(2)
    sort_chunk(1)
    weights_of(tiles, 2 * tiles)
    of_partner(weights_of)
    gather(3)
    mate_copy(0, 1 - odd).wait_recv()
    of_mate(weights_of)
    sort_chunk(2)
    sort_chunk(3)
    apply_weights(tiles, 2 * tiles)
    of_partner(apply_weights)
    mate_copy(1, 1 - odd).wait_recv()
    of_mate(apply_weights)

    for i, (a, slot) in enumerate(chunks):
        for_targets(i, lambda copy: copy.wait_send())
        if slot == 1:
            far_copy(a, far_owner, me, mine).wait_send()
            mate_copy(a, odd).wait_send()

        @pl.when(has_partner)
        def _():
            swap_copy(i, side).wait_send()

    @pl.when(has_partner)
    def _():
        order_copy(own_slot).wait_send()


def fused_on_device(n, anomalies, innovations, sort_order, obs_error):
    rows, total = anomalies.shape
    panel = total // n
    members = rows * n
    tiles = panel // TILE
    blocks = panel // SORT
    half = n // 2
    bf16, f32 = jnp.bfloat16, jnp.float32
    hbm = pl.BlockSpec(memory_space=pltpu.HBM)
    dma = pltpu.SemaphoreType.DMA
    return pl.pallas_call(
        functools.partial(kernel, n),
        out_shape=jax.ShapeDtypeStruct((panel, members), f32),
        in_specs=[hbm] * 4,
        out_specs=pl.BlockSpec(memory_space=pltpu.VMEM),
        scratch_shapes=[
            pltpu.VMEM((2, n // 4, 2, 2, rows, 2 * panel), bf16),
            pltpu.VMEM((members, 3 * panel), bf16),
            pltpu.VMEM((3 * panel, members), bf16),
            pltpu.VMEM((panel, members), bf16),
            pltpu.VMEM((tiles, TILE, (2 * tiles + 1) * TILE), bf16),
            pltpu.VMEM((TILE, (2 * tiles + 1) * TILE), f32),
            pltpu.VMEM((2, blocks, SORT), jnp.int32),
            pltpu.VMEM((blocks, SORT), f32),
            pltpu.VMEM((2, blocks, SORT, SORT), bf16),
            pltpu.VMEM((2, blocks, SORT, SORT), bf16),
            pltpu.VMEM((panel, SORT), f32),
            dma((4, half)),
            dma((4, half)),
            dma((4,)),
            dma((2,)),
            dma((2, half)),
            dma((4,)),
            dma((4,)),
            dma((2,)),
            dma((2,)),
            dma((2,)),
            dma((2,)),
        ],
        compiler_params=pltpu.CompilerParams(
            collective_id=0, has_side_effects=True, vmem_limit_bytes=63 * 1024 * 1024
        ),
    )(
        anomalies,
        innovations,
        sort_order.reshape(blocks, SORT),
        obs_error.reshape(blocks, SORT),
    )


def on_device(n, anomalies, innovations, sort_order, obs_error):
    rows, total = anomalies.shape
    if n % 4 or rows % 16 or (total // n) % (2 * TILE) or (rows * n) % TILE:
        return plain_on_device(anomalies, innovations, sort_order, obs_error)
    return fused_on_device(n, anomalies, innovations, sort_order, obs_error)


def solution(mesh):
    return jax.shard_map(
        functools.partial(on_device, mesh.shape["obs"]),
        mesh=mesh,
        in_specs=(
            P(("grp", "obs"), None),
            P(("grp", "obs"), None),
            P(("grp", "obs")),
            P(("grp", "obs")),
        ),
        out_specs=P(("grp", "obs"), None),
        check_vma=False,
    )
```
